512 devices in a mesh: section: 32 (over x, z_lo), dp: 16 (over z_hi, y, core).
Axes of the slice: x: 4, y: 4, z: 16 (z_hi: 2, z_lo: 8; z = z_hi * 8 + z_lo), core: 2. Of those that a mesh axis runs over, the one named last changes fastest.
Arguments:
- memory: bfloat16 [2048, 2048], P('dp', 'section'), may hold values from -6 to 6
- queries: bfloat16 [32, 2048, 2048], P('section', 'dp'), may hold values from -6 to 6
- values: bfloat16 [32, 2048, 2048], P('section', 'dp'), may hold values from -6 to 6
- out_grad: bfloat16 [32, 2048, 2048], P('section', 'dp'), may hold values from -6 to 6
- key_weight: bfloat16 [32, 2048, 2048], P('section', 'dp'), may hold values from -0.125 to 0.125
- first_codes: bfloat16 [32, 2048, 2048], P('section', 'dp'), may hold values from -1 to 1
- first_scales: float32 [32, 16, 2048], P('section', None, 'dp'), may hold values from 0.5 to 5
- second_codes: bfloat16 [32, 2048, 2048], P('section', 'dp'), may hold values from 0.049804688 to 1
- second_scales: float32 [32, 16, 2048], P('section', None, 'dp'), may hold values from 2 to 20
Outputs:
- memory_grad: float32 [2048, 2048], P('dp', 'section')
- update: bfloat16 [32, 2048, 2048], P('section', 'dp')
- new_first_codes: bfloat16 [32, 2048, 2048], P('section', 'dp')
- new_first_scales: float32 [32, 16, 2048], P('section', None, 'dp')
- new_second_codes: bfloat16 [32, 2048, 2048], P('section', 'dp')
- new_second_scales: float32 [32, 16, 2048], P('section', None, 'dp')
The draws below stay inside these ranges and needn't reach their ends.
All inputs are finite; a program needn't handle non-finite values. Where the reference program divides by a largest or mean magnitude, that divisor is 1e-20 or more.
Results may differ from the reference program's by a relative error of at most 0.012.
Values may be sent and summed in bfloat16 or wider, within the bound.
A program may use at most 64 MiB of HBM per device.

```python
import math
import jax
import jax.numpy as jnp
from jax import lax

DW = 2048
HEADS = 8
HD = 256
TQ = 128
TK = 128
INNER = 2048
NB = 16
N_SECTION = 32
N_DP = 16


def steps_of(key, shape, shards, least, largest):
    level = 1.0
    for dim, parts in shards:
        heights = jax.random.uniform(jax.random.fold_in(jax.random.fold_in(key, 6), dim), (parts,), jnp.float32, least / len(shards), largest / len(shards))
        level = level * jnp.repeat(jnp.exp(heights), shape[dim] // parts).reshape((-1,) + (1,) * (len(shape) - 1 - dim))
    return level


def bell_draw(rng, extent, spread, limit, split=(), kind=jnp.bfloat16):
    level = steps_of(rng, extent, split, -0.22, 0.18) if split else 1.0
    result = jax.random.normal(rng, extent, jnp.float32) * spread * level
    return jnp.minimum(jnp.maximum(result, -limit), limit).astype(kind)


def setup_inputs(seed: int = 0) -> dict:
    seeds = jax.random.split(jax.random.key(seed), 10)
    return {
        "memory": bell_draw(seeds[0], (N_DP * TK, DW), 1.0, 6.0, ((0, 16), (1, 32))),
        "queries": bell_draw(seeds[1], (N_SECTION, N_DP * TQ, INNER), 1.0, 6.0, ((0, 32), (1, 16))),
        "values": bell_draw(seeds[2], (N_SECTION, N_DP * TK, INNER), 1.0, 6.0, ((0, 32), (1, 16))),
        "out_grad": bell_draw(seeds[3], (N_SECTION, N_DP * TQ, INNER), 1.0, 6.0, ((0, 32), (1, 16))),
        "key_weight": bell_draw(seeds[4], (N_SECTION, DW, INNER), DW ** -0.5, 0.125, ((0, 32), (1, 16))),
        "first_codes": jnp.clip(jax.random.uniform(seeds[5], (N_SECTION, DW, INNER), jnp.float32, -1.0, 1.0) * steps_of(seeds[5], (N_SECTION, DW, INNER), ((0, 32), (1, 16)), -0.4, 0.0), -1.0, 1.0).astype(jnp.bfloat16),
        "first_scales": jnp.clip(jnp.exp(math.log(5.0) - 2.3025851 * jax.random.uniform(seeds[6], (N_SECTION, NB, DW), jnp.float32) ** steps_of(seeds[6], (N_SECTION, NB, DW), ((0, 32), (2, 16)), -0.2, 0.2)), 0.5, 5.0),
        "second_codes": jnp.clip(0.049804688 + 0.9501953 * jax.random.uniform(seeds[7], (N_SECTION, DW, INNER), jnp.float32) ** steps_of(seeds[7], (N_SECTION, DW, INNER), ((0, 32), (1, 16)), -0.2, 0.2), 0.049804688, 1.0).astype(jnp.bfloat16),
        "second_scales": jnp.clip(jnp.exp(math.log(20.0) - 2.3025851 * jax.random.uniform(seeds[8], (N_SECTION, NB, DW), jnp.float32) ** steps_of(seeds[8], (N_SECTION, NB, DW), ((0, 32), (2, 16)), -0.2, 0.2)), 2.0, 20.0),
    }


beta_one = 0.9
beta_two = 0.95
corr_one = 1.0 - 0.9 ** 10
corr_two = 1.0 - 0.95 ** 10

def sequence_grad(key_rows, queries, values, out_grad):
    scale = HD ** (-0.5)
    key_heads = key_rows.reshape(TK, HEADS, HD).astype(jnp.float32)
    query_heads = queries.reshape(TQ, HEADS, HD).astype(jnp.float32)
    value_heads = values.reshape(TK, HEADS, HD).astype(jnp.float32)
    grad_heads = out_grad.reshape(TQ, HEADS, HD).astype(jnp.float32)
    scores = jnp.einsum('khd,qhd->hkq', key_heads, query_heads) * scale
    expon = jnp.exp(scores)
    probs = expon / lax.optimization_barrier(jnp.sum(expon, axis=1, keepdims=True))
    prob_grad = jnp.einsum('khd,qhd->hkq', value_heads, grad_heads)
    score_grad = (probs * (prob_grad - lax.optimization_barrier(jnp.sum(probs * prob_grad, axis=1, keepdims=True))) * scale).astype(jnp.bfloat16)
    key_grad = jnp.einsum('hkq,qhd->khd', score_grad.astype(jnp.float32), query_heads)
    return key_grad.reshape(TK, HEADS * HD).astype(jnp.bfloat16)

def adam_step(weight_grad, first_codes, first_scales, second_codes, second_scales):
    row_count = weight_grad.shape[0]
    blocks = first_scales.shape[0]
    first_prev = first_codes.astype(jnp.float32).reshape(row_count, blocks, -1) * first_scales.T[:, :, None]
    second_prev = second_codes.astype(jnp.float32).reshape(row_count, blocks, -1) * second_scales.T[:, :, None]
    grad_blocks = weight_grad.reshape(row_count, blocks, -1)
    first = beta_one * first_prev + (1.0 - beta_one) * grad_blocks
    second = beta_two * second_prev + (1.0 - beta_two) * grad_blocks * grad_blocks
    update = first / corr_one / (jnp.sqrt(second / corr_two) + 1e-08)
    first_max = lax.optimization_barrier(jnp.max(jnp.abs(first), axis=2)) + 1e-06
    second_max = lax.optimization_barrier(jnp.max(second, axis=2)) + 1e-06
    first_new = (first / first_max[:, :, None]).astype(jnp.bfloat16)
    second_new = (second / second_max[:, :, None]).astype(jnp.bfloat16)
    return (update.reshape(row_count, -1).astype(jnp.bfloat16), first_new.reshape(row_count, -1), first_max.T, second_new.reshape(row_count, -1), second_max.T)

def reference(memory, queries, values, out_grad, key_weight, first_codes, first_scales, second_codes, second_scales):

    def layer(total, inputs):
        weight, query_rows, value_rows, grad_rows, codes_one, scales_one, codes_two, scales_two = inputs
        key_rows = jnp.dot(memory, weight, preferred_element_type=jnp.float32).astype(jnp.bfloat16)
        key_grad = jax.vmap(sequence_grad)(key_rows.reshape(N_DP, TK, -1), query_rows.reshape(N_DP, TQ, -1), value_rows.reshape(N_DP, TK, -1), grad_rows.reshape(N_DP, TQ, -1))
        key_grad = key_grad.reshape(N_DP * TK, -1)
        total = total + jnp.dot(key_grad, weight.T, preferred_element_type=jnp.float32)
        weight_grad = jnp.dot(memory.T, key_grad, preferred_element_type=jnp.float32)
        return (total, adam_step(weight_grad, codes_one, scales_one, codes_two, scales_two))
    start = jnp.zeros((N_DP * TK, DW), jnp.float32)
    memory_grad, outputs = lax.scan(layer, start, (key_weight, queries, values, out_grad, first_codes, first_scales, second_codes, second_scales))
    return (memory_grad, outputs[0], outputs[1], outputs[2], outputs[3], outputs[4])
```

```python
import functools

import jax
import jax.numpy as jnp
from jax import lax
from jax.experimental import pallas as pl
from jax.experimental.pallas import tpu as pltpu
from jax.sharding import PartitionSpec as P

HEADS = 8
HD = 256
SCALE = HD ** (-0.5)
MESH = pl.DeviceIdType.MESH

beta_one = 0.9
beta_two = 0.95
corr_one = 1.0 - 0.9**10
corr_two = 1.0 - 0.95**10

GRAD_LAG = 8
NT = (((1,), (1,)), ((), ()))
NN = (((1,), (0,)), ((), ()))


def dot(a, b, dims=NN):
    return lax.dot_general(a, b, dims, preferred_element_type=jnp.float32)


def block_place(q):
    return (q % 2) * 8 + (q // 8) * 4 + (q // 2) % 4


def rows(start, size):
    return pl.ds(pl.multiple_of(start, size), size)


def wait_bytes(ref, sem):
    pltpu.make_async_copy(ref, ref, sem).wait()


def kernel(
    memory_ref, queries_ref, values_ref, out_grad_ref, weight_ref,
    codes_one_ref, scales_one_ref, codes_two_ref, scales_two_ref,
    memory_grad_ref, update_ref, new_one_ref, new_scale_one_ref, new_two_ref, new_scale_two_ref,
    weights, grads, slots, feats, encoded, feat_rows, terms, halves_out, halves_in, parts_out, parts_in,
    scale_cols_one, scale_cols_two, new_cols_one, new_cols_two,
    small_send, small_recv, w_send, w_z, w_y, w_core, g_send, g_z, g_y, g_core,
):
    s = lax.axis_index("section")
    q = lax.axis_index("dp")
    x, zl = lax.div(s, 8), lax.rem(s, 8)
    zh, y, core = lax.div(q, 8), lax.rem(lax.div(q, 2), 4), lax.rem(q, 2)

    far = (s, lax.rem(q + 8, 16))
    sibling = (s, q + 1 - 2 * core)
    along_y = [(s, zh * 8 + lax.rem(y + k, 4) * 2 + core) for k in (1, 3, 2)]
    along_x = [(lax.rem(s + 8 * k, 32), q) for k in (1, 3, 2)]
    along_z = [(x * 8 + lax.rem(zl + k, 8), q) for k in range(1, 8)]
    turn_to = (lax.rem(2 * q + lax.rem(s, 2) + 8, 32), lax.div(s, 2))
    turn_from = (2 * q + lax.rem(s, 2), lax.div(lax.rem(s + 24, 32), 2))

    barrier = pltpu.get_barrier_semaphore()
    partners = [far, sibling, *along_y, *along_x, *along_z, turn_from]
    for partner in partners:
        pl.semaphore_signal(barrier, inc=1, device_id=partner, device_id_type=MESH)
    pl.semaphore_wait(barrier, len(partners))

    def send(src, dst, send_sem, recv_sem, device):
        pltpu.make_async_remote_copy(
            src_ref=src, dst_ref=dst, send_sem=send_sem, recv_sem=recv_sem,
            device_id=device, device_id_type=MESH,
        ).start()

    own = rows((core * 8 + zh * 4 + y) * 128, 128)
    other = rows((core * 8 + (1 - zh) * 4 + y) * 128, 128)
    mine = rows(core * 1024, 1024)
    here = rows(s * 64, 64)
    column = rows(x * 512, 512)

    slots[here, :] = memory_ref[...].astype(jnp.float32).T.astype(jnp.bfloat16)
    turn_slot = rows(turn_to[0] * 64, 64)
    send(slots.at[here], feats.at[turn_slot], small_send.at[0], small_recv.at[0], turn_to)
    for device in along_z:
        send(slots.at[here], slots.at[here], small_send.at[1], small_recv.at[1], device)

    for h in range(HEADS):
        weights[h, own, :] = weight_ref[0, :, h * HD : (h + 1) * HD]

    def own_weights(h, _):
        piece = weights.at[h, own]
        send(piece, piece, w_send.at[h], w_z.at[h], far)
        for device in along_y:
            send(piece, piece, w_send.at[h], w_y.at[h], device)
        return 0

    lax.fori_loop(0, HEADS, own_weights, 0)

    wait_bytes(feats.at[pl.ds(0, 64)], small_recv.at[0])
    for device in along_z:
        send(feats.at[here], feats.at[here], small_send.at[2], small_recv.at[2], device)
    wait_bytes(slots.at[pl.ds(0, 448)], small_recv.at[1])
    for device in along_x:
        send(slots.at[column], slots.at[column], small_send.at[3], small_recv.at[3], device)

    scale_cols_one[...] = jnp.zeros((128, 128), jnp.float32)
    scale_cols_two[...] = jnp.zeros((128, 128), jnp.float32)
    scale_cols_one[0:16, :] = scales_one_ref[0]
    scale_cols_two[0:16, :] = scales_two_ref[0]
    scale_cols_one[...] = scale_cols_one[...].T
    scale_cols_two[...] = scale_cols_two[...].T
    new_cols_one[...] = jnp.zeros((128, 128), jnp.float32)
    new_cols_two[...] = jnp.zeros((128, 128), jnp.float32)
    terms[...] = jnp.zeros((2048, 128), jnp.float32)

    wait_bytes(feats.at[pl.ds(0, 448)], small_recv.at[2])
    for device in along_x:
        send(feats.at[column], feats.at[column], small_send.at[4], small_recv.at[4], device)

    wait_bytes(slots.at[pl.ds(0, 1536)], small_recv.at[3])
    for block in range(16):
        place = block_place(block)
        encoded[:, place * 128 : (place + 1) * 128] = (
            slots[block * 128 : (block + 1) * 128, :].astype(jnp.float32).T.astype(jnp.bfloat16)
        )

    def relay(buf, send_sem, z_sem, y_sem, h):
        wait_bytes(buf.at[h, pl.ds(0, 128)], z_sem.at[h])
        piece = buf.at[h, other]
        for device in along_y:
            send(piece, piece, send_sem.at[h], y_sem.at[h], device)

    def to_sibling(buf, send_sem, y_sem, core_sem, h):
        wait_bytes(buf.at[h, pl.ds(0, 768)], y_sem.at[h])
        piece = buf.at[h, mine]
        send(piece, piece, send_sem.at[h], core_sem.at[h], sibling)

    def key_gradient(h):
        wait_bytes(weights.at[h, pl.ds(0, 1024)], w_core.at[h])
        columns = rows(h * HD, HD)
        head_queries = queries_ref[0, :, columns]
        key_rows = dot(encoded[...], weights[h]).astype(jnp.bfloat16)
        expon = jnp.exp(dot(key_rows, head_queries, NT) * SCALE)
        probs = expon / jnp.sum(expon, axis=0, keepdims=True)
        prob_grad = dot(values_ref[0, :, columns], out_grad_ref[0, :, columns], NT)
        score_grad = probs * (prob_grad - jnp.sum(probs * prob_grad, axis=0, keepdims=True)) * SCALE
        key_grad = dot(score_grad.astype(jnp.bfloat16), head_queries).astype(jnp.bfloat16)
        grads[h, own, :] = key_grad
        piece = grads.at[h, own]
        send(piece, piece, g_send.at[h], g_z.at[h], far)
        for device in along_y:
            send(piece, piece, g_send.at[h], g_y.at[h], device)
        terms[...] += dot(weights[h], key_grad, NT)

    lane = lax.broadcasted_iota(jnp.int32, (128, 128), 1)

    def adam(h):
        wait_bytes(grads.at[h, pl.ds(0, 1024)], g_core.at[h])
        weight_grad = dot(feat_rows[...], grads[h])
        for part in range(HD // 128):
            block = h * (HD // 128) + part
            columns = rows(block * 128, 128)
            grad = weight_grad[:, part * 128 : (part + 1) * 128]
            chosen = lane == block
            scale_one = jnp.sum(jnp.where(chosen, scale_cols_one[...], 0.0), axis=1, keepdims=True)
            scale_two = jnp.sum(jnp.where(chosen, scale_cols_two[...], 0.0), axis=1, keepdims=True)
            first_prev = codes_one_ref[0, :, columns].astype(jnp.float32) * scale_one
            second_prev = codes_two_ref[0, :, columns].astype(jnp.float32) * scale_two
            first = beta_one * first_prev + (1.0 - beta_one) * grad
            second = beta_two * second_prev + (1.0 - beta_two) * grad * grad
            update = first / corr_one / (jnp.sqrt(second / corr_two) + 1e-08)
            first_max = jnp.max(jnp.abs(first), axis=1, keepdims=True) + 1e-06
            second_max = jnp.max(second, axis=1, keepdims=True) + 1e-06
            update_ref[0, :, columns] = update.astype(jnp.bfloat16)
            new_one_ref[0, :, columns] = (first / first_max).astype(jnp.bfloat16)
            new_two_ref[0, :, columns] = (second / second_max).astype(jnp.bfloat16)
            new_cols_one[...] = jnp.where(chosen, first_max, new_cols_one[...])
            new_cols_two[...] = jnp.where(chosen, second_max, new_cols_two[...])

    def memory_terms():
        for block in range(16):
            place = block_place(block)
            halves_out[block * 128 : (block + 1) * 128, :] = (
                terms[place * 128 : (place + 1) * 128, :].astype(jnp.bfloat16)
            )
        for k, device in zip((1, 3, 2), along_x):
            part = rows(lax.rem(x + k, 4) * 512, 512)
            send(halves_out.at[part], halves_in.at[k - 1], small_send.at[5], small_recv.at[5], device)

        wait_bytes(feats.at[pl.ds(0, 1536)], small_recv.at[4])
        for block in range(16):
            place = block_place(block)
            at = ((block + 4) % 16) * 128
            feat_rows[:, place * 128 : (place + 1) * 128] = feats[at : at + 128, :]

    def memory_columns():
        wait_bytes(halves_out.at[pl.ds(0, 1536)], small_recv.at[5])
        total = halves_out[column, :].astype(jnp.float32)
        for k in range(3):
            total += halves_in[k].astype(jnp.float32)
        parts_out[...] = total.astype(jnp.bfloat16)
        for k, device in zip(range(1, 8), along_z):
            part = rows(lax.rem(zl + k, 8) * 64, 64)
            send(parts_out.at[part], parts_in.at[k - 1], small_send.at[6], small_recv.at[6], device)

    def memory_result():
        wait_bytes(parts_out.at[pl.ds(0, 448)], small_recv.at[6])
        total = parts_out[rows(zl * 64, 64), :].astype(jnp.float32)
        for k in range(7):
            total += parts_in[k].astype(jnp.float32)
        memory_grad_ref[...] = total

    def step(t, _):
        @pl.when(t < HEADS)
        def _():
            relay(weights, w_send, w_z, w_y, t)

        @pl.when((t >= 1) & (t < HEADS + 1))
        def _():
            to_sibling(weights, w_send, w_y, w_core, t - 1)

        @pl.when((t >= 2) & (t < HEADS + 2))
        def _():
            key_gradient(t - 2)

        @pl.when(t == HEADS + 1)
        def _():
            memory_terms()

        @pl.when(t == HEADS + 3)
        def _():
            memory_columns()

        @pl.when(t == HEADS + 6)
        def _():
            memory_result()

        u = t - GRAD_LAG

        @pl.when((u >= 0) & (u < HEADS))
        def _():
            relay(grads, g_send, g_z, g_y, u)

        @pl.when((u >= 1) & (u < HEADS + 1))
        def _():
            to_sibling(grads, g_send, g_y, g_core, u - 1)

        @pl.when((u >= 2) & (u < HEADS + 2))
        def _():
            adam(u - 2)

        return 0

    lax.fori_loop(0, GRAD_LAG + HEADS + 2, step, 0)
    new_scale_one_ref[0] = new_cols_one[...].T[0:16, :]
    new_scale_two_ref[0] = new_cols_two[...].T[0:16, :]

    def sent(h, _):
        wait_bytes(weights.at[h, pl.ds(0, 1920)], w_send.at[h])
        wait_bytes(grads.at[h, pl.ds(0, 1920)], g_send.at[h])
        return 0

    lax.fori_loop(0, HEADS, sent, 0)
    for k, count in enumerate((64, 448, 448, 1536, 1536, 1536, 448)):
        wait_bytes(slots.at[pl.ds(0, count)], small_send.at[k])


def local(memory, queries, values, out_grad, key_weight, codes_one, scales_one, codes_two, scales_two):
    bf16, f32 = jnp.bfloat16, jnp.float32
    vmem = pl.BlockSpec(memory_space=pltpu.VMEM)
    sems = pltpu.SemaphoreType.DMA
    outs = pl.pallas_call(
        kernel,
        out_shape=(
            jax.ShapeDtypeStruct((64, 128), f32),
            jax.ShapeDtypeStruct((1, 128, 2048), bf16),
            jax.ShapeDtypeStruct((1, 128, 2048), bf16),
            jax.ShapeDtypeStruct((1, 16, 128), f32),
            jax.ShapeDtypeStruct((1, 128, 2048), bf16),
            jax.ShapeDtypeStruct((1, 16, 128), f32),
        ),
        in_specs=[vmem] * 9,
        out_specs=(vmem,) * 6,
        scratch_shapes=[
            pltpu.VMEM((HEADS, 2048, HD), bf16),
            pltpu.VMEM((HEADS, 2048, HD), bf16),
            pltpu.VMEM((2048, 128), bf16),
            pltpu.VMEM((2048, 128), bf16),
            pltpu.VMEM((128, 2048), bf16),
            pltpu.VMEM((128, 2048), bf16),
            pltpu.VMEM((2048, 128), f32),
            pltpu.VMEM((2048, 128), bf16),
            pltpu.VMEM((3, 512, 128), bf16),
            pltpu.VMEM((512, 128), bf16),
            pltpu.VMEM((7, 64, 128), bf16),
            pltpu.VMEM((128, 128), f32),
            pltpu.VMEM((128, 128), f32),
            pltpu.VMEM((128, 128), f32),
            pltpu.VMEM((128, 128), f32),
            sems((7,)),
            sems((7,)),
        ]
        + [sems((HEADS,))] * 8,
        compiler_params=pltpu.CompilerParams(
            collective_id=0, has_side_effects=True, vmem_limit_bytes=48 << 20
        ),
        name="projection_backward",
    )(memory, queries, values, out_grad, key_weight, codes_one, scales_one, codes_two, scales_two)
    return (outs[0].T, *outs[1:])


def solution(mesh):
    return jax.shard_map(
        local,
        mesh=mesh,
        in_specs=(
            P("dp", "section"),
            P("section", "dp", None),
            P("section", "dp", None),
            P("section", "dp", None),
            P("section", "dp", None),
            P("section", "dp", None),
            P("section", None, "dp"),
            P("section", "dp", None),
            P("section", None, "dp"),
        ),
        out_specs=(
            P("dp", "section"),
            P("section", "dp", None),
            P("section", "dp", None),
            P("section", None, "dp"),
            P("section", "dp", None),
            P("section", None, "dp"),
        ),
        check_vma=False,
    )
```

```python
import functools

import jax
import jax.numpy as jnp
from jax import lax
from jax.experimental import pallas as pl
from jax.experimental.pallas import tpu as pltpu
from jax.sharding import PartitionSpec as P

HEADS = 8
HD = 256
SCALE = HD ** (-0.5)
MESH = pl.DeviceIdType.MESH

beta_one = 0.9
beta_two = 0.95
corr_one = 1.0 - 0.9**10
corr_two = 1.0 - 0.95**10

GRAD_LAG = 8
FIRST, SECOND, THIRD, OWN_AHEAD = 8, 8, 8, 8
KEY_LAG = 3
NT = (((1,), (1,)), ((), ()))
NN = (((1,), (0,)), ((), ()))


def dot(a, b, dims=NN):
    return lax.dot_general(a, b, dims, preferred_element_type=jnp.float32)


def block_place(q):
    return (q % 2) * 8 + (q // 8) * 4 + (q // 2) % 4


def reversed_bits(z):
    return (z % 2) * 4 + z // 2 % 2 * 2 + z // 4


def rows(start, size):
    return pl.ds(pl.multiple_of(start, size), size)


def wait_bytes(ref, sem):
    pltpu.make_async_copy(ref, ref, sem).wait()


def writer(*refs):
    count = len(refs) // 2
    sem = refs[-1]
    copies = [pltpu.make_async_copy(refs[k], refs[count + k], sem.at[k]) for k in range(count)]
    for copy in copies:
        copy.start()
    for copy in copies:
        copy.wait()


def kernel(
    memory_hbm, queries_hbm, values_hbm, out_grad_hbm, weight_hbm,
    codes_one_hbm, scales_one_ref, codes_two_hbm, scales_two_ref,
    memory_grad_ref, update_ref, new_one_ref, new_scale_one_ref, new_two_ref, new_scale_two_ref,
    queries_ref, values_ref, out_grad_ref, codes_one_ref, codes_two_ref,
    weights, grads, slots, feats, encoded, feat_rows, terms, halves_out, halves_in, totals, parts_out, parts_in,
    scale_cols_one, scale_cols_two, new_cols_one, new_cols_two,
    load_sem, turn_send, turn_recv, column_send, column_recv, x_send, x_recv,
    half_send, half_recv, part_send, part_recv,
    wo_send, wo_behind, w_send, w_z, w_behind, w_rest, w_core,
    g_send, go_behind, go_rest, go_core, g_z, g_behind, g_rest, g_core,
):
    s = lax.axis_index("section")
    q = lax.axis_index("dp")
    x, zl = lax.div(s, 8), lax.rem(s, 8)
    zh, y, core = lax.div(q, 8), lax.rem(lax.div(q, 2), 4), lax.rem(q, 2)
    y_ahead, y_behind = lax.rem(y + 5 - 2 * core, 4), lax.rem(y + 3 + 2 * core, 4)

    far = (s, lax.rem(q + 8, 16))
    sibling = (s, q + 1 - 2 * core)
    ahead = (s, zh * 8 + y_ahead * 2 + core)
    behind = (s, zh * 8 + y_behind * 2 + core)
    along_x = [(lax.rem(s + 8 * k, 32), q) for k in (1, 3, 2)]
    half_bit, quarter_bit, unit_bit = lax.div(zl, 4), lax.rem(lax.div(zl, 2), 2), lax.rem(zl, 2)
    pairs = [(s + 4 - 8 * half_bit, q), (s + 2 - 4 * quarter_bit, q), (s + 1 - 2 * unit_bit, q)]
    turn_to = (lax.rem(2 * q + lax.rem(s, 2) + 8, 32), lax.div(s, 2))
    turn_from = (2 * q + lax.rem(s, 2), lax.div(lax.rem(s + 24, 32), 2))

    first_half, second_half = core * 8 + zh * 4, core * 8 + (1 - zh) * 4
    own, own_behind = rows((first_half + y) * 128, 128), rows((first_half + y_behind) * 128, 128)
    other, other_behind = rows((second_half + y) * 128, 128), rows((second_half + y_behind) * 128, 128)
    mine = rows(core * 1024, 1024)
    own_half, other_half = rows(first_half * 128, 512), rows(second_half * 128, 512)
    column = rows(x * 512, 512)
    place = unit_bit * 4 + quarter_bit * 2 + half_bit
    groups = [rows((x * 8 + place) * 64, 64), rows((x * 4 + lax.div(place, 2)) * 128, 128), rows((x * 2 + unit_bit) * 256, 256)]
    here = groups[0]

    load_memory = pltpu.make_async_copy(memory_hbm, slots.at[here], load_sem.at[0])
    load_memory.start()

    def load_weight(h):
        return pltpu.make_async_copy(
            weight_hbm.at[0, :, h * HD : (h + 1) * HD], weights.at[h, own], load_sem.at[6 + h]
        )

    for h in range(HEADS):
        load_weight(h).start()
    loads = [
        pltpu.make_async_copy(src, dst, load_sem.at[1 + k])
        for k, (src, dst) in enumerate(
            (
                (queries_hbm, queries_ref), (values_hbm, values_ref), (out_grad_hbm, out_grad_ref),
                (codes_one_hbm, codes_one_ref), (codes_two_hbm, codes_two_ref),
            )
        )
    ]
    for load in loads:
        load.start()

    barrier = pltpu.get_barrier_semaphore()
    partners = [far, sibling, ahead, behind, *along_x, *pairs, turn_from]
    for partner in partners:
        pl.semaphore_signal(barrier, inc=1, device_id=partner, device_id_type=MESH)
    pl.semaphore_wait(barrier, len(partners))

    def send(src, dst, send_sem, recv_sem, device):
        pltpu.make_async_remote_copy(
            src_ref=src, dst_ref=dst, send_sem=send_sem, recv_sem=recv_sem,
            device_id=device, device_id_type=MESH,
        ).start()

    load_memory.wait()

    def along_z(buf, base, k):
        piece = buf.at[groups[k]]
        send(piece, piece, column_send.at[base + k], column_recv.at[base + k], pairs[k])

    def along_z_next(buf, base, k):
        wait_bytes(buf.at[pl.ds(0, 64 << (k - 1))], column_recv.at[base + k - 1])
        along_z(buf, base, k)

    along_z(slots, 0, 0)
    send(slots.at[here], feats.at[rows((lax.div(turn_to[0], 8) * 8 + reversed_bits(lax.rem(turn_to[0], 8))) * 64, 64)], turn_send.at[0], turn_recv.at[0], turn_to)

    def weight_columns():
        wait_bytes(feats.at[pl.ds(0, 64)], turn_recv.at[0])
        along_z(feats, 3, 0)

    def far_weights(h):
        columns = rows(h * HD, HD)
        send(weight_hbm.at[0, :, columns], weights.at[h, own], w_send.at[h], w_z.at[h], far)

    def spread(buf, piece, send_sem, behind_sem, rest_sem, h):
        piece = buf.at[h, piece]
        send(piece, piece, send_sem.at[h], behind_sem.at[h], ahead)
        send(piece, piece, send_sem.at[h], rest_sem.at[h], behind)

    def own_weights(h):
        spread(weights, own, wo_send, wo_behind, w_rest, h)

    def columns_across(buf, base, k):
        wait_bytes(buf.at[pl.ds(0, 256)], column_recv.at[base + 2])
        for device in along_x:
            send(buf.at[column], buf.at[column], x_send.at[k], x_recv.at[k], device)

    along_z_next(slots, 0, 1)
    for h in range(FIRST):
        far_weights(h)
    weight_columns()
    for h in range(HEADS):
        load_weight(h).wait()
    for h in range(OWN_AHEAD):
        own_weights(h)
    for h in range(FIRST, SECOND):
        far_weights(h)

    def section_block(buf, section):
        low = (section // 8 * 8 + reversed_bits(section % 8)) * 64
        return buf[low : low + 64, :]

    def weight_features():
        wait_bytes(feats.at[pl.ds(0, 1536)], x_recv.at[1])
        for block in range(16):
            place = block_place(block)
            for half in range(2):
                feat_rows[half * 64 : (half + 1) * 64, place * 128 : (place + 1) * 128] = section_block(
                    feats, (2 * block + half + 8) % 32
                )

    def encode():
        wait_bytes(slots.at[pl.ds(0, 1536)], x_recv.at[0])
        for block in range(16):
            place = block_place(block)
            features = jnp.concatenate([section_block(slots, 2 * block + half) for half in range(2)], axis=0)
            encoded[:, place * 128 : (place + 1) * 128] = features.astype(jnp.float32).T.astype(jnp.bfloat16)
        scale_cols_one[...] = jnp.zeros((128, 128), jnp.float32)
        scale_cols_two[...] = jnp.zeros((128, 128), jnp.float32)
        scale_cols_one[0:16, :] = scales_one_ref[0]
        scale_cols_two[0:16, :] = scales_two_ref[0]
        scale_cols_one[...] = scale_cols_one[...].T
        scale_cols_two[...] = scale_cols_two[...].T
        new_cols_one[...] = jnp.zeros((128, 128), jnp.float32)
        new_cols_two[...] = jnp.zeros((128, 128), jnp.float32)
        terms[...] = jnp.zeros((2048, 128), jnp.float32)
        for load in loads:
            load.wait()

    def relay(buf, piece, send_sem, behind_sem, rest_sem, h):
        wait_bytes(buf.at[h, pl.ds(0, 128)], behind_sem.at[h])
        piece = buf.at[h, piece]
        send(piece, piece, send_sem.at[h], rest_sem.at[h], ahead)

    def to_sibling(buf, half, count, send_sem, rest_sem, core_sem, h):
        wait_bytes(buf.at[h, pl.ds(0, count)], rest_sem.at[h])
        piece = buf.at[h, half]
        send(piece, piece, send_sem.at[h], core_sem.at[h], sibling)

    def key_gradient(h):
        wait_bytes(weights.at[h, pl.ds(0, 1024)], w_core.at[h])
        columns = rows(h * HD, HD)
        head_queries = queries_ref[0, :, columns]
        key_rows = dot(encoded[...], weights[h]).astype(jnp.bfloat16)
        expon = jnp.exp(dot(key_rows, head_queries, NT) * SCALE)
        probs = expon / jnp.sum(expon, axis=0, keepdims=True)
        prob_grad = dot(values_ref[0, :, columns], out_grad_ref[0, :, columns], NT)
        score_grad = probs * (prob_grad - jnp.sum(probs * prob_grad, axis=0, keepdims=True)) * SCALE
        key_grad = dot(score_grad.astype(jnp.bfloat16), head_queries).astype(jnp.bfloat16)
        grads[h, own, :] = key_grad
        piece = grads.at[h, own]
        send(piece, piece, g_send.at[h], g_z.at[h], far)
        spread(grads, own, g_send, go_behind, go_rest, h)
        terms[...] += dot(weights[h], key_grad, NT)

    lane = lax.broadcasted_iota(jnp.int32, (128, 128), 1)

    def adam(h):
        wait_bytes(grads.at[h, pl.ds(0, 512)], go_core.at[h])
        wait_bytes(grads.at[h, pl.ds(0, 512)], g_core.at[h])
        weight_grad = dot(feat_rows[...], grads[h])
        for part in range(HD // 128):
            block = h * (HD // 128) + part
            columns = rows(block * 128, 128)
            grad = weight_grad[:, part * 128 : (part + 1) * 128]
            chosen = lane == block
            scale_one = jnp.sum(jnp.where(chosen, scale_cols_one[...], 0.0), axis=1, keepdims=True)
            scale_two = jnp.sum(jnp.where(chosen, scale_cols_two[...], 0.0), axis=1, keepdims=True)
            first_prev = codes_one_ref[0, :, columns].astype(jnp.float32) * scale_one
            second_prev = codes_two_ref[0, :, columns].astype(jnp.float32) * scale_two
            first = beta_one * first_prev + (1.0 - beta_one) * grad
            second = beta_two * second_prev + (1.0 - beta_two) * grad * grad
            update = first / corr_one / (jnp.sqrt(second / corr_two) + 1e-08)
            first_max = jnp.max(jnp.abs(first), axis=1, keepdims=True) + 1e-06
            second_max = jnp.max(second, axis=1, keepdims=True) + 1e-06
            update_ref[0, :, columns] = update.astype(jnp.bfloat16)
            new_one_ref[0, :, columns] = (first / first_max).astype(jnp.bfloat16)
            new_two_ref[0, :, columns] = (second / second_max).astype(jnp.bfloat16)
            new_cols_one[...] = jnp.where(chosen, first_max, new_cols_one[...])
            new_cols_two[...] = jnp.where(chosen, second_max, new_cols_two[...])

    def memory_terms():
        for block in range(16):
            place = block_place(block)
            halves_out[block * 128 : (block + 1) * 128, :] = (
                terms[place * 128 : (place + 1) * 128, :].astype(jnp.bfloat16)
            )
        for k, device in zip((1, 3, 2), along_x):
            part = rows(lax.rem(x + k, 4) * 512, 512)
            send(halves_out.at[part], halves_in.at[k - 1], half_send.at[0], half_recv.at[0], device)

    def exchange_parts(k):
        size = 256 >> k
        low = rows(other_blocks[k] * size, size)
        parts_out[low, :] = totals[low, :].astype(jnp.bfloat16)
        landing = parts_in.at[pl.ds(512 - 2 * size, size)]
        send(parts_out.at[low], landing, part_send.at[k], part_recv.at[k], pairs[2 - k])

    def add_parts(k):
        size = 256 >> k
        landing = pl.ds(512 - 2 * size, size)
        wait_bytes(parts_in.at[landing], part_recv.at[k])
        low = rows(kept_blocks[k] * size, size)
        totals[low, :] += parts_in[landing, :].astype(jnp.float32)

    kept_blocks = [unit_bit, unit_bit * 2 + quarter_bit, place]
    other_blocks = [1 - unit_bit, unit_bit * 2 + 1 - quarter_bit, unit_bit * 4 + quarter_bit * 2 + 1 - half_bit]

    def memory_columns():
        wait_bytes(halves_out.at[pl.ds(0, 1536)], half_recv.at[0])
        total = halves_out[column, :].astype(jnp.float32)
        for k in range(3):
            total += halves_in[k].astype(jnp.float32)
        for z in range(8):
            low = reversed_bits(z) * 64
            totals[low : low + 64, :] = total[z * 64 : (z + 1) * 64, :]
        exchange_parts(0)

    def memory_parts(k):
        add_parts(k)
        exchange_parts(k + 1)

    def memory_result():
        add_parts(2)
        memory_grad_ref[...] = totals[rows(place * 64, 64), :]

    def far_range(first, last):
        for h in range(first, last):
            far_weights(h)

    def step(t, _):
        def at(first, count, act):
            @pl.when((t >= first) & (t < first + count))
            def _():
                act(t - first)

        k, g = KEY_LAG, GRAD_LAG
        at(0, HEADS, lambda h: spread_far(weights, w_send, w_z, w_behind, w_rest, h))
        at(0, HEADS - OWN_AHEAD, lambda h: own_weights(h + OWN_AHEAD))
        at(0, 1, lambda h: along_z_next(slots, 0, 2))
        at(0, 1, lambda h: along_z_next(feats, 3, 1))
        at(0, 1, lambda h: far_range(SECOND, THIRD))
        at(1, 1, lambda h: columns_across(slots, 0, 0))
        at(1, 1, lambda h: along_z_next(feats, 3, 2))
        at(1, 1, lambda h: far_range(THIRD, HEADS))
        at(2, 1, lambda h: columns_across(feats, 3, 1))
        at(0, HEADS, lambda h: relay(weights, own_behind, w_send, wo_behind, w_rest, h))
        at(1, HEADS, lambda h: relay(weights, other_behind, w_send, w_behind, w_rest, h))
        at(2, HEADS, lambda h: to_sibling(weights, mine, 512, w_send, w_rest, w_core, h))
        at(k, 1, lambda h: encode())
        at(k, HEADS, key_gradient)
        at(k + HEADS - 1, 1, lambda h: memory_terms())
        at(k + 1, HEADS, lambda h: relay(grads, own_behind, g_send, go_behind, go_rest, h))
        at(k + 2, HEADS, lambda h: to_sibling(grads, own_half, 256, g_send, go_rest, go_core, h))
        at(g, HEADS, lambda h: spread_far(grads, g_send, g_z, g_behind, g_rest, h))
        at(g + 1, HEADS, lambda h: relay(grads, other_behind, g_send, g_behind, g_rest, h))
        at(g + 2, HEADS, lambda h: to_sibling(grads, other_half, 256, g_send, g_rest, g_core, h))
        at(g + 3, 1, lambda h: weight_features())
        at(g + 3, HEADS, adam)
        at(k + HEADS + 1, 1, lambda h: memory_columns())
        at(k + HEADS + 2, 1, lambda h: memory_parts(0))
        at(k + HEADS + 3, 1, lambda h: memory_parts(1))
        at(k + HEADS + 4, 1, lambda h: memory_result())
        return 0

    def spread_far(buf, send_sem, z_sem, behind_sem, rest_sem, h):
        wait_bytes(buf.at[h, pl.ds(0, 128)], z_sem.at[h])
        spread(buf, other, send_sem, behind_sem, rest_sem, h)

    lax.fori_loop(0, GRAD_LAG + HEADS + 3, step, 0)
    new_scale_one_ref[0] = new_cols_one[...].T[0:16, :]
    new_scale_two_ref[0] = new_cols_two[...].T[0:16, :]

    def sent(h, _):
        wait_bytes(weights.at[h, pl.ds(0, 1664)], w_send.at[h])
        wait_bytes(weights.at[h, pl.ds(0, 256)], wo_send.at[h])
        wait_bytes(grads.at[h, pl.ds(0, 1920)], g_send.at[h])
        return 0

    lax.fori_loop(0, HEADS, sent, 0)
    wait_bytes(slots.at[pl.ds(0, 64)], turn_send.at[0])
    wait_bytes(slots.at[pl.ds(0, 1536)], x_send.at[0])
    wait_bytes(slots.at[pl.ds(0, 1536)], x_send.at[1])
    for k in range(3):
        wait_bytes(slots.at[pl.ds(0, 64 << k)], column_send.at[k])
        wait_bytes(slots.at[pl.ds(0, 64 << k)], column_send.at[3 + k])
        wait_bytes(parts_out.at[pl.ds(0, 256 >> k)], part_send.at[k])
    wait_bytes(halves_out.at[pl.ds(0, 1536)], half_send.at[0])


def local(memory, queries, values, out_grad, key_weight, codes_one, scales_one, codes_two, scales_two):
    bf16, f32 = jnp.bfloat16, jnp.float32
    vmem, anywhere = pl.BlockSpec(memory_space=pltpu.VMEM), pl.BlockSpec(memory_space=pl.ANY)
    sems = pltpu.SemaphoreType.DMA
    one, each = sems((1,)), sems((HEADS,))
    shapes = (
        jax.ShapeDtypeStruct((64, 128), f32),
        jax.ShapeDtypeStruct((1, 128, 2048), bf16),
        jax.ShapeDtypeStruct((1, 128, 2048), bf16),
        jax.ShapeDtypeStruct((1, 16, 128), f32),
        jax.ShapeDtypeStruct((1, 128, 2048), bf16),
        jax.ShapeDtypeStruct((1, 16, 128), f32),
    )
    outs = pl.pallas_call(
        kernel,
        out_shape=shapes,
        in_specs=[anywhere] * 6 + [vmem, anywhere, vmem],
        out_specs=(vmem,) * 6,
        scratch_shapes=[pltpu.VMEM((1, 128, 2048), bf16)] * 5
        + [
            pltpu.VMEM((HEADS, 2048, HD), bf16),
            pltpu.VMEM((HEADS, 2048, HD), bf16),
            pltpu.VMEM((2048, 128), bf16),
            pltpu.VMEM((2048, 128), bf16),
            pltpu.VMEM((128, 2048), bf16),
            pltpu.VMEM((128, 2048), bf16),
            pltpu.VMEM((2048, 128), f32),
            pltpu.VMEM((2048, 128), bf16),
            pltpu.VMEM((3, 512, 128), bf16),
            pltpu.VMEM((512, 128), f32),
            pltpu.VMEM((512, 128), bf16),
            pltpu.VMEM((512, 128), bf16),
        ]
        + [pltpu.VMEM((128, 128), f32)] * 4
        + [sems((6 + HEADS,)), one, one, sems((6,)), sems((6,)), sems((2,)), sems((2,)), one, one, sems((3,)), sems((3,))]
        + [each] * 7
        + [each] * 8,
        compiler_params=pltpu.CompilerParams(
            collective_id=0, has_side_effects=True, vmem_limit_bytes=56 << 20
        ),
        name="projection_backward",
    )(memory.T, queries, values, out_grad, key_weight, codes_one, scales_one, codes_two, scales_two)
    outs = pl.pallas_call(
        writer,
        out_shape=shapes,
        in_specs=[vmem] * 6,
        out_specs=(anywhere,) * 6,
        scratch_shapes=[sems((6,))],
        name="write_results",
    )(*outs)
    return (outs[0].T, *outs[1:])


def solution(mesh):
    return jax.shard_map(
        local,
        mesh=mesh,
        in_specs=(
            P("dp", "section"),
            P("section", "dp", None),
            P("section", "dp", None),
            P("section", "dp", None),
            P("section", "dp", None),
            P("section", "dp", None),
            P("section", None, "dp"),
            P("section", "dp", None),
            P("section", None, "dp"),
        ),
        out_specs=(
            P("dp", "section"),
            P("section", "dp", None),
            P("section", "dp", None),
            P("section", None, "dp"),
            P("section", "dp", None),
            P("section", None, "dp"),
        ),
        check_vma=False,
    )
```

```python
import functools

import jax
import jax.numpy as jnp
from jax import lax
from jax.experimental import pallas as pl
from jax.experimental.pallas import tpu as pltpu
from jax.sharding import PartitionSpec as P

HEADS = 8
HD = 256
SCALE = HD ** (-0.5)
MESH = pl.DeviceIdType.MESH

beta_one = 0.9
beta_two = 0.95
corr_one = 1.0 - 0.9**10
corr_two = 1.0 - 0.95**10

GRAD_LAG = 6
FIRST, SECOND, THIRD, OWN_AHEAD = 8, 8, 8, 8
KEY_LAG = 4
FAR_LAG = 1
NT = (((1,), (1,)), ((), ()))
NN = (((1,), (0,)), ((), ()))


def dot(a, b, dims=NN):
    return lax.dot_general(a, b, dims, preferred_element_type=jnp.float32)


def block_place(q):
    return (q % 2) * 8 + (q // 8) * 4 + (q // 2) % 4


def reversed_bits(z):
    return (z % 2) * 4 + z // 2 % 2 * 2 + z // 4


def rows(start, size):
    return pl.ds(pl.multiple_of(start, size), size)


def wait_bytes(ref, sem):
    pltpu.make_async_copy(ref, ref, sem).wait()


def writer(*refs):
    count = len(refs) // 2
    sem = refs[-1]
    copies = [pltpu.make_async_copy(refs[k], refs[count + k], sem.at[k]) for k in range(count)]
    for copy in copies:
        copy.start()
    for copy in copies:
        copy.wait()


def kernel(
    memory_hbm, queries_hbm, values_hbm, out_grad_hbm, weight_hbm,
    codes_one_hbm, scales_one_ref, codes_two_hbm, scales_two_ref,
    memory_grad_ref, update_ref, new_one_ref, new_scale_one_ref, new_two_ref, new_scale_two_ref,
    queries_ref, values_ref, out_grad_ref, codes_one_ref, codes_two_ref,
    weights, grads, w_passing, g_passing, slots, feats, encoded, feat_rows, terms, halves_out, halves_in, totals, parts_out, parts_in,
    scale_cols_one, scale_cols_two, new_cols_one, new_cols_two,
    load_sem, turn_send, turn_recv, column_send, column_recv, x_send, x_recv,
    half_send, half_recv, part_send, part_recv,
    wo_send, wo_behind, w_send, w_z, w_behind, w_rest, w_core,
    g_send, go_behind, go_rest, go_core, g_z, g_behind, g_rest, g_core,
    w_up, w_down, g_up, g_down,
):
    s = lax.axis_index("section")
    q = lax.axis_index("dp")
    x, zl = lax.div(s, 8), lax.rem(s, 8)
    zh, y, core = lax.div(q, 8), lax.rem(lax.div(q, 2), 4), lax.rem(q, 2)
    y_ahead, y_behind = lax.rem(y + 5 - 2 * core, 4), lax.rem(y + 3 + 2 * core, 4)

    z = zh * 8 + zl

    def at_z(z):
        return (x * 8 + lax.rem(z, 8), lax.div(z, 8) * 8 + lax.rem(q, 8))

    z_up, z_down = lax.rem(z + 4, 16), lax.rem(z + 12, 16)
    up, down = at_z(z_up), at_z(z_down)
    sibling = (s, q + 1 - 2 * core)
    ahead = (s, zh * 8 + y_ahead * 2 + core)
    behind = (s, zh * 8 + y_behind * 2 + core)
    along_x = [(lax.rem(s + 8 * k, 32), q) for k in (1, 3, 2)]
    half_bit, quarter_bit, unit_bit = lax.div(zl, 4), lax.rem(lax.div(zl, 2), 2), lax.rem(zl, 2)
    pairs = [(s + 4 - 8 * half_bit, q), (s + 2 - 4 * quarter_bit, q), (s + 1 - 2 * unit_bit, q)]
    turn_to = (lax.rem(2 * q + lax.rem(s, 2) + 8, 32), lax.div(s, 2))
    turn_from = (2 * q + lax.rem(s, 2), lax.div(lax.rem(s + 24, 32), 2))

    first_half, second_half = core * 8 + zh * 4, core * 8 + (1 - zh) * 4
    own, own_behind = rows((first_half + y) * 128, 128), rows((first_half + y_behind) * 128, 128)
    other, other_behind = rows((second_half + y) * 128, 128), rows((second_half + y_behind) * 128, 128)
    mine = rows(core * 1024, 1024)
    own_low, own_high = rows((first_half + y) * 128, 64), rows((first_half + y) * 128 + 64, 64)
    passing_low = rows((core * 8 + lax.div(z_down, 8) * 4 + y) * 128, 64)
    passing_high = rows((core * 8 + lax.div(z_up, 8) * 4 + y) * 128 + 64, 64)
    low, high = pl.ds(0, 64), pl.ds(64, 64)
    own_half, other_half = rows(first_half * 128, 512), rows(second_half * 128, 512)
    column = rows(x * 512, 512)
    place = unit_bit * 4 + quarter_bit * 2 + half_bit
    groups = [rows((x * 8 + place) * 64, 64), rows((x * 4 + lax.div(place, 2)) * 128, 128), rows((x * 2 + unit_bit) * 256, 256)]
    here = groups[0]

    load_memory = pltpu.make_async_copy(memory_hbm, slots.at[here], load_sem.at[0])
    load_memory.start()

    def load_weight(h):
        return pltpu.make_async_copy(
            weight_hbm.at[0, :, h * HD : (h + 1) * HD], weights.at[h, own], load_sem.at[6 + h]
        )

    for h in range(HEADS):
        load_weight(h).start()
    loads = [
        pltpu.make_async_copy(src, dst, load_sem.at[1 + k])
        for k, (src, dst) in enumerate(
            (
                (queries_hbm, queries_ref), (values_hbm, values_ref), (out_grad_hbm, out_grad_ref),
                (codes_one_hbm, codes_one_ref), (codes_two_hbm, codes_two_ref),
            )
        )
    ]
    for load in loads:
        load.start()

    barrier = pltpu.get_barrier_semaphore()
    partners = [up, down, sibling, ahead, behind, *along_x, *pairs, turn_from]
    for partner in partners:
        pl.semaphore_signal(barrier, inc=1, device_id=partner, device_id_type=MESH)
    pl.semaphore_wait(barrier, len(partners))

    def send(src, dst, send_sem, recv_sem, device):
        pltpu.make_async_remote_copy(
            src_ref=src, dst_ref=dst, send_sem=send_sem, recv_sem=recv_sem,
            device_id=device, device_id_type=MESH,
        ).start()

    load_memory.wait()

    def along_z(buf, base, k):
        piece = buf.at[groups[k]]
        send(piece, piece, column_send.at[base + k], column_recv.at[base + k], pairs[k])

    def along_z_next(buf, base, k):
        wait_bytes(buf.at[pl.ds(0, 64 << (k - 1))], column_recv.at[base + k - 1])
        along_z(buf, base, k)

    along_z(slots, 0, 0)
    send(slots.at[here], feats.at[rows((lax.div(turn_to[0], 8) * 8 + reversed_bits(lax.rem(turn_to[0], 8))) * 64, 64)], turn_send.at[0], turn_recv.at[0], turn_to)

    def weight_columns():
        wait_bytes(feats.at[pl.ds(0, 64)], turn_recv.at[0])
        along_z(feats, 3, 0)

    def far_weights(h):
        columns = rows(h * HD, HD)
        send(weight_hbm.at[0, low, columns], w_passing.at[h, low], w_send.at[h], w_up.at[h], up)
        send(weight_hbm.at[0, high, columns], w_passing.at[h, high], w_send.at[h], w_down.at[h], down)

    def pass_on(buf, passing, send_sem, up_sem, down_sem, z_sem, h):
        wait_bytes(passing.at[h, low], up_sem.at[h])
        send(passing.at[h, low], buf.at[h, passing_low], send_sem.at[h], z_sem.at[h], up)
        wait_bytes(passing.at[h, high], down_sem.at[h])
        send(passing.at[h, high], buf.at[h, passing_high], send_sem.at[h], z_sem.at[h], down)

    def pass_weights(h):
        pass_on(weights, w_passing, w_send, w_up, w_down, w_z, h)

    def spread(buf, piece, send_sem, behind_sem, rest_sem, h):
        piece = buf.at[h, piece]
        send(piece, piece, send_sem.at[h], behind_sem.at[h], ahead)
        send(piece, piece, send_sem.at[h], rest_sem.at[h], behind)

    def own_weights(h):
        spread(weights, own, wo_send, wo_behind, w_rest, h)

    def columns_across(buf, base, k):
        wait_bytes(buf.at[pl.ds(0, 256)], column_recv.at[base + 2])
        for device in along_x:
            send(buf.at[column], buf.at[column], x_send.at[k], x_recv.at[k], device)

    along_z_next(slots, 0, 1)
    for h in range(FIRST):
        far_weights(h)
    for h in range(HEADS):
        load_weight(h).wait()
    for h in range(OWN_AHEAD):
        own_weights(h)
    for h in range(FIRST, SECOND):
        far_weights(h)

    def section_block(buf, section):
        low = (section // 8 * 8 + reversed_bits(section % 8)) * 64
        return buf[low : low + 64, :]

    def weight_features():
        wait_bytes(feats.at[pl.ds(0, 1536)], x_recv.at[1])
        for block in range(16):
            place = block_place(block)
            for half in range(2):
                feat_rows[half * 64 : (half + 1) * 64, place * 128 : (place + 1) * 128] = section_block(
                    feats, (2 * block + half + 8) % 32
                )

    def encode():
        wait_bytes(slots.at[pl.ds(0, 1536)], x_recv.at[0])
        for block in range(16):
            place = block_place(block)
            features = jnp.concatenate([section_block(slots, 2 * block + half) for half in range(2)], axis=0)
            encoded[:, place * 128 : (place + 1) * 128] = features.astype(jnp.float32).T.astype(jnp.bfloat16)
        scale_cols_one[...] = jnp.zeros((128, 128), jnp.float32)
        scale_cols_two[...] = jnp.zeros((128, 128), jnp.float32)
        scale_cols_one[0:16, :] = scales_one_ref[0]
        scale_cols_two[0:16, :] = scales_two_ref[0]
        scale_cols_one[...] = scale_cols_one[...].T
        scale_cols_two[...] = scale_cols_two[...].T
        new_cols_one[...] = jnp.zeros((128, 128), jnp.float32)
        new_cols_two[...] = jnp.zeros((128, 128), jnp.float32)
        terms[...] = jnp.zeros((2048, 128), jnp.float32)
        for load in loads:
            load.wait()

    def relay(buf, piece, send_sem, behind_sem, rest_sem, h):
        wait_bytes(buf.at[h, pl.ds(0, 128)], behind_sem.at[h])
        piece = buf.at[h, piece]
        send(piece, piece, send_sem.at[h], rest_sem.at[h], ahead)

    def to_sibling(buf, half, count, send_sem, rest_sem, core_sem, h):
        wait_bytes(buf.at[h, pl.ds(0, count)], rest_sem.at[h])
        piece = buf.at[h, half]
        send(piece, piece, send_sem.at[h], core_sem.at[h], sibling)

    def key_gradient(h):
        wait_bytes(weights.at[h, pl.ds(0, 1024)], w_core.at[h])
        columns = rows(h * HD, HD)
        head_queries = queries_ref[0, :, columns]
        key_rows = dot(encoded[...], weights[h]).astype(jnp.bfloat16)
        expon = jnp.exp(dot(key_rows, head_queries, NT) * SCALE)
        probs = expon / jnp.sum(expon, axis=0, keepdims=True)
        prob_grad = dot(values_ref[0, :, columns], out_grad_ref[0, :, columns], NT)
        score_grad = probs * (prob_grad - jnp.sum(probs * prob_grad, axis=0, keepdims=True)) * SCALE
        key_grad = dot(score_grad.astype(jnp.bfloat16), head_queries).astype(jnp.bfloat16)
        grads[h, own, :] = key_grad
        send(grads.at[h, own_low], g_passing.at[h, low], g_send.at[h], g_up.at[h], up)
        send(grads.at[h, own_high], g_passing.at[h, high], g_send.at[h], g_down.at[h], down)
        spread(grads, own, g_send, go_behind, go_rest, h)
        terms[...] += dot(weights[h], key_grad, NT)

    lane = lax.broadcasted_iota(jnp.int32, (128, 128), 1)

    def adam(h):
        wait_bytes(grads.at[h, pl.ds(0, 512)], go_core.at[h])
        wait_bytes(grads.at[h, pl.ds(0, 512)], g_core.at[h])
        weight_grad = dot(feat_rows[...], grads[h])
        for part in range(HD // 128):
            block = h * (HD // 128) + part
            columns = rows(block * 128, 128)
            grad = weight_grad[:, part * 128 : (part + 1) * 128]
            chosen = lane == block
            scale_one = jnp.sum(jnp.where(chosen, scale_cols_one[...], 0.0), axis=1, keepdims=True)
            scale_two = jnp.sum(jnp.where(chosen, scale_cols_two[...], 0.0), axis=1, keepdims=True)
            first_prev = codes_one_ref[0, :, columns].astype(jnp.float32) * scale_one
            second_prev = codes_two_ref[0, :, columns].astype(jnp.float32) * scale_two
            first = beta_one * first_prev + (1.0 - beta_one) * grad
            second = beta_two * second_prev + (1.0 - beta_two) * grad * grad
            update = first / corr_one / (jnp.sqrt(second / corr_two) + 1e-08)
            first_max = jnp.max(jnp.abs(first), axis=1, keepdims=True) + 1e-06
            second_max = jnp.max(second, axis=1, keepdims=True) + 1e-06
            update_ref[0, :, columns] = update.astype(jnp.bfloat16)
            new_one_ref[0, :, columns] = (first / first_max).astype(jnp.bfloat16)
            new_two_ref[0, :, columns] = (second / second_max).astype(jnp.bfloat16)
            new_cols_one[...] = jnp.where(chosen, first_max, new_cols_one[...])
            new_cols_two[...] = jnp.where(chosen, second_max, new_cols_two[...])

    def memory_terms():
        for block in range(16):
            place = block_place(block)
            halves_out[block * 128 : (block + 1) * 128, :] = (
                terms[place * 128 : (place + 1) * 128, :].astype(jnp.bfloat16)
            )
        for k, device in zip((1, 3, 2), along_x):
            part = rows(lax.rem(x + k, 4) * 512, 512)
            send(halves_out.at[part], halves_in.at[k - 1], half_send.at[0], half_recv.at[0], device)

    def exchange_parts(k):
        size = 256 >> k
        low = rows(other_blocks[k] * size, size)
        parts_out[low, :] = totals[low, :].astype(jnp.bfloat16)
        landing = parts_in.at[pl.ds(512 - 2 * size, size)]
        send(parts_out.at[low], landing, part_send.at[k], part_recv.at[k], pairs[2 - k])

    def add_parts(k):
        size = 256 >> k
        landing = pl.ds(512 - 2 * size, size)
        wait_bytes(parts_in.at[landing], part_recv.at[k])
        low = rows(kept_blocks[k] * size, size)
        totals[low, :] += parts_in[landing, :].astype(jnp.float32)

    kept_blocks = [unit_bit, unit_bit * 2 + quarter_bit, place]
    other_blocks = [1 - unit_bit, unit_bit * 2 + 1 - quarter_bit, unit_bit * 4 + quarter_bit * 2 + 1 - half_bit]

    def memory_columns():
        wait_bytes(halves_out.at[pl.ds(0, 1536)], half_recv.at[0])
        total = halves_out[column, :].astype(jnp.float32)
        for k in range(3):
            total += halves_in[k].astype(jnp.float32)
        for z in range(8):
            low = reversed_bits(z) * 64
            totals[low : low + 64, :] = total[z * 64 : (z + 1) * 64, :]
        exchange_parts(0)

    def memory_parts(k):
        add_parts(k)
        exchange_parts(k + 1)

    def memory_result():
        add_parts(2)
        memory_grad_ref[...] = totals[rows(place * 64, 64), :]

    def far_range(first, last):
        for h in range(first, last):
            far_weights(h)

    def step(t, _):
        def at(first, count, act):
            @pl.when((t >= first) & (t < first + count))
            def _():
                act(t - first)

        k, g = KEY_LAG, GRAD_LAG
        f = FAR_LAG
        at(0, HEADS - 2, lambda h: pass_weights(h + 2))
        at(g, HEADS, lambda h: pass_on(grads, g_passing, g_send, g_up, g_down, g_z, h))
        at(f, HEADS, lambda h: spread_far(weights, w_send, w_z, w_behind, w_rest, h))
        at(0, HEADS - OWN_AHEAD, lambda h: own_weights(h + OWN_AHEAD))
        at(0, 1, lambda h: along_z_next(slots, 0, 2))
        at(0, 1, lambda h: weight_columns())
        at(2, 1, lambda h: along_z_next(feats, 3, 1))
        at(0, 1, lambda h: far_range(SECOND, THIRD))
        at(1, 1, lambda h: columns_across(slots, 0, 0))
        at(4, 1, lambda h: along_z_next(feats, 3, 2))
        at(1, 1, lambda h: far_range(THIRD, HEADS))
        at(6, 1, lambda h: columns_across(feats, 3, 1))
        at(0, HEADS, lambda h: relay(weights, own_behind, w_send, wo_behind, w_rest, h))
        at(f + 1, HEADS, lambda h: relay(weights, other_behind, w_send, w_behind, w_rest, h))
        at(f + 2, HEADS, lambda h: to_sibling(weights, mine, 512, w_send, w_rest, w_core, h))
        at(k, 1, lambda h: encode())
        at(k, HEADS, key_gradient)
        at(k + HEADS - 1, 1, lambda h: memory_terms())
        at(k + 1, HEADS, lambda h: relay(grads, own_behind, g_send, go_behind, go_rest, h))
        at(k + 2, HEADS, lambda h: to_sibling(grads, own_half, 256, g_send, go_rest, go_core, h))
        at(g + f, HEADS, lambda h: spread_far(grads, g_send, g_z, g_behind, g_rest, h))
        at(g + f + 1, HEADS, lambda h: relay(grads, other_behind, g_send, g_behind, g_rest, h))
        at(g + f + 2, HEADS, lambda h: to_sibling(grads, other_half, 256, g_send, g_rest, g_core, h))
        at(g + f + 3, 1, lambda h: weight_features())
        at(g + f + 3, HEADS, adam)
        at(k + HEADS + 1, 1, lambda h: memory_columns())
        at(k + HEADS + 2, 1, lambda h: memory_parts(0))
        at(k + HEADS + 3, 1, lambda h: memory_parts(1))
        at(k + HEADS + 4, 1, lambda h: memory_result())
        return 0

    def spread_far(buf, send_sem, z_sem, behind_sem, rest_sem, h):
        wait_bytes(buf.at[h, pl.ds(0, 128)], z_sem.at[h])
        spread(buf, other, send_sem, behind_sem, rest_sem, h)

    pass_weights(0)
    pass_weights(1)
    lax.fori_loop(0, GRAD_LAG + FAR_LAG + HEADS + 3, step, 0)
    new_scale_one_ref[0] = new_cols_one[...].T[0:16, :]
    new_scale_two_ref[0] = new_cols_two[...].T[0:16, :]

    def sent(h, _):
        wait_bytes(weights.at[h, pl.ds(0, 1792)], w_send.at[h])
        wait_bytes(weights.at[h, pl.ds(0, 256)], wo_send.at[h])
        wait_bytes(grads.at[h, pl.ds(0, 2048)], g_send.at[h])
        return 0

    lax.fori_loop(0, HEADS, sent, 0)
    wait_bytes(slots.at[pl.ds(0, 64)], turn_send.at[0])
    wait_bytes(slots.at[pl.ds(0, 1536)], x_send.at[0])
    wait_bytes(slots.at[pl.ds(0, 1536)], x_send.at[1])
    for k in range(3):
        wait_bytes(slots.at[pl.ds(0, 64 << k)], column_send.at[k])
        wait_bytes(slots.at[pl.ds(0, 64 << k)], column_send.at[3 + k])
        wait_bytes(parts_out.at[pl.ds(0, 256 >> k)], part_send.at[k])
    wait_bytes(halves_out.at[pl.ds(0, 1536)], half_send.at[0])


def local(memory, queries, values, out_grad, key_weight, codes_one, scales_one, codes_two, scales_two):
    bf16, f32 = jnp.bfloat16, jnp.float32
    vmem, anywhere = pl.BlockSpec(memory_space=pltpu.VMEM), pl.BlockSpec(memory_space=pl.ANY)
    sems = pltpu.SemaphoreType.DMA
    one, each = sems((1,)), sems((HEADS,))
    shapes = (
        jax.ShapeDtypeStruct((64, 128), f32),
        jax.ShapeDtypeStruct((1, 128, 2048), bf16),
        jax.ShapeDtypeStruct((1, 128, 2048), bf16),
        jax.ShapeDtypeStruct((1, 16, 128), f32),
        jax.ShapeDtypeStruct((1, 128, 2048), bf16),
        jax.ShapeDtypeStruct((1, 16, 128), f32),
    )
    outs = pl.pallas_call(
        kernel,
        out_shape=shapes,
        in_specs=[anywhere] * 6 + [vmem, anywhere, vmem],
        out_specs=(vmem,) * 6,
        scratch_shapes=[pltpu.VMEM((1, 128, 2048), bf16)] * 5
        + [
            pltpu.VMEM((HEADS, 2048, HD), bf16),
            pltpu.VMEM((HEADS, 2048, HD), bf16),
            pltpu.VMEM((HEADS, 128, HD), bf16),
            pltpu.VMEM((HEADS, 128, HD), bf16),
            pltpu.VMEM((2048, 128), bf16),
            pltpu.VMEM((2048, 128), bf16),
            pltpu.VMEM((128, 2048), bf16),
            pltpu.VMEM((128, 2048), bf16),
            pltpu.VMEM((2048, 128), f32),
            pltpu.VMEM((2048, 128), bf16),
            pltpu.VMEM((3, 512, 128), bf16),
            pltpu.VMEM((512, 128), f32),
            pltpu.VMEM((512, 128), bf16),
            pltpu.VMEM((512, 128), bf16),
        ]
        + [pltpu.VMEM((128, 128), f32)] * 4
        + [sems((6 + HEADS,)), one, one, sems((6,)), sems((6,)), sems((2,)), sems((2,)), one, one, sems((3,)), sems((3,))]
        + [each] * 7
        + [each] * 12,
        compiler_params=pltpu.CompilerParams(
            collective_id=0, has_side_effects=True, vmem_limit_bytes=56 << 20
        ),
        name="projection_backward",
    )(memory.T, queries, values, out_grad, key_weight, codes_one, scales_one, codes_two, scales_two)
    outs = pl.pallas_call(
        writer,
        out_shape=shapes,
        in_specs=[vmem] * 6,
        out_specs=(anywhere,) * 6,
        scratch_shapes=[sems((6,))],
        name="write_results",
    )(*outs)
    return (outs[0].T, *outs[1:])


def solution(mesh):
    return jax.shard_map(
        local,
        mesh=mesh,
        in_specs=(
            P("dp", "section"),
            P("section", "dp", None),
            P("section", "dp", None),
            P("section", "dp", None),
            P("section", "dp", None),
            P("section", "dp", None),
            P("section", None, "dp"),
            P("section", "dp", None),
            P("section", None, "dp"),
        ),
        out_specs=(
            P("dp", "section"),
            P("section", "dp", None),
            P("section", "dp", None),
            P("section", None, "dp"),
            P("section", "dp", None),
            P("section", None, "dp"),
        ),
        check_vma=False,
    )
```

```python
import functools

import jax
import jax.numpy as jnp
from jax import lax
from jax.experimental import pallas as pl
from jax.experimental.pallas import tpu as pltpu
from jax.sharding import PartitionSpec as P

HEADS = 8
HD = 256
SCALE = HD ** (-0.5)
MESH = pl.DeviceIdType.MESH

beta_one = 0.9
beta_two = 0.95
corr_one = 1.0 - 0.9**10
corr_two = 1.0 - 0.95**10

GRAD_LAG = 6
FIRST, SECOND, THIRD, OWN_AHEAD = 8, 8, 8, 8
KEY_LAG = 4
FAR_LAG = 1
NT = (((1,), (1,)), ((), ()))
NN = (((1,), (0,)), ((), ()))


def dot(a, b, dims=NN):
    return lax.dot_general(a, b, dims, preferred_element_type=jnp.float32)


def block_place(q):
    return (q % 2) * 8 + (q // 8) * 4 + (q // 2) % 4


def reversed_bits(z):
    return (z % 2) * 4 + z // 2 % 2 * 2 + z // 4


def rows(start, size):
    return pl.ds(pl.multiple_of(start, size), size)


def wait_bytes(ref, sem):
    pltpu.make_async_copy(ref, ref, sem).wait()


def writer(*refs):
    count = len(refs) // 2
    sem = refs[-1]
    copies = [pltpu.make_async_copy(refs[k], refs[count + k], sem.at[k]) for k in range(count)]
    for copy in copies:
        copy.start()
    for copy in copies:
        copy.wait()


def kernel(
    memory_hbm, queries_hbm, values_hbm, out_grad_hbm, weight_hbm,
    codes_one_hbm, scales_one_ref, codes_two_hbm, scales_two_ref,
    memory_grad_ref, update_ref, new_one_ref, new_scale_one_ref, new_two_ref, new_scale_two_ref,
    queries_ref, values_ref, out_grad_ref, codes_one_ref, codes_two_ref,
    weights, grads, w_passing, g_passing, slots, feats, encoded, feat_rows, terms, halves_out, halves_in, totals, parts_out, parts_in,
    scale_cols_one, scale_cols_two, new_cols_one, new_cols_two,
    load_sem, turn_send, turn_recv, column_send, column_recv, x_send, x_recv,
    half_send, half_recv, part_send, part_recv,
    wo_send, wo_behind, w_send, w_z, w_behind, w_rest, w_core,
    g_send, go_behind, go_rest, go_core, g_z, g_rest, g_core,
    w_up, w_down, g_up, g_down,
):
    s = lax.axis_index("section")
    q = lax.axis_index("dp")
    x, zl = lax.div(s, 8), lax.rem(s, 8)
    zh, y, core = lax.div(q, 8), lax.rem(lax.div(q, 2), 4), lax.rem(q, 2)
    y_ahead, y_behind = lax.rem(y + 5 - 2 * core, 4), lax.rem(y + 3 + 2 * core, 4)

    z = zh * 8 + zl

    def at_z(z):
        return (x * 8 + lax.rem(z, 8), lax.div(z, 8) * 8 + lax.rem(q, 8))

    z_up, z_down = lax.rem(z + 4, 16), lax.rem(z + 12, 16)
    up, down = at_z(z_up), at_z(z_down)
    sibling = (s, q + 1 - 2 * core)
    ahead = (s, zh * 8 + y_ahead * 2 + core)
    behind = (s, zh * 8 + y_behind * 2 + core)
    opposite = (s, zh * 8 + lax.rem(y + 2, 4) * 2 + core)
    along_x = [(lax.rem(s + 8 * k, 32), q) for k in (1, 3, 2)]
    half_bit, quarter_bit, unit_bit = lax.div(zl, 4), lax.rem(lax.div(zl, 2), 2), lax.rem(zl, 2)
    pairs = [(s + 4 - 8 * half_bit, q), (s + 2 - 4 * quarter_bit, q), (s + 1 - 2 * unit_bit, q)]
    turn_to = (lax.rem(2 * q + lax.rem(s, 2) + 8, 32), lax.div(s, 2))
    turn_from = (2 * q + lax.rem(s, 2), lax.div(lax.rem(s + 24, 32), 2))

    first_half, second_half = core * 8 + zh * 4, core * 8 + (1 - zh) * 4
    own, own_behind = rows((first_half + y) * 128, 128), rows((first_half + y_behind) * 128, 128)
    other, other_behind = rows((second_half + y) * 128, 128), rows((second_half + y_behind) * 128, 128)
    mine = rows(core * 1024, 1024)
    own_low, own_high = rows((first_half + y) * 128, 64), rows((first_half + y) * 128 + 64, 64)
    passing_low = rows((core * 8 + lax.div(z_down, 8) * 4 + y) * 128, 64)
    passing_high = rows((core * 8 + lax.div(z_up, 8) * 4 + y) * 128 + 64, 64)
    low, high = pl.ds(0, 64), pl.ds(64, 64)
    own_half, other_half = rows(first_half * 128, 512), rows(second_half * 128, 512)
    column = rows(x * 512, 512)
    place = unit_bit * 4 + quarter_bit * 2 + half_bit
    groups = [rows((x * 8 + place) * 64, 64), rows((x * 4 + lax.div(place, 2)) * 128, 128), rows((x * 2 + unit_bit) * 256, 256)]
    here = groups[0]

    load_memory = pltpu.make_async_copy(memory_hbm, slots.at[here], load_sem.at[0])
    load_memory.start()

    def load_weight(h):
        return pltpu.make_async_copy(
            weight_hbm.at[0, :, h * HD : (h + 1) * HD], weights.at[h, own], load_sem.at[6 + h]
        )

    for h in range(HEADS):
        load_weight(h).start()
    loads = [
        pltpu.make_async_copy(src, dst, load_sem.at[1 + k])
        for k, (src, dst) in enumerate(
            (
                (queries_hbm, queries_ref), (values_hbm, values_ref), (out_grad_hbm, out_grad_ref),
                (codes_one_hbm, codes_one_ref), (codes_two_hbm, codes_two_ref),
            )
        )
    ]
    for load in loads:
        load.start()

    barrier = pltpu.get_barrier_semaphore()
    partners = [up, down, sibling, ahead, behind, opposite, *along_x, *pairs, turn_from]
    for partner in partners:
        pl.semaphore_signal(barrier, inc=1, device_id=partner, device_id_type=MESH)
    pl.semaphore_wait(barrier, len(partners))

    def send(src, dst, send_sem, recv_sem, device):
        pltpu.make_async_remote_copy(
            src_ref=src, dst_ref=dst, send_sem=send_sem, recv_sem=recv_sem,
            device_id=device, device_id_type=MESH,
        ).start()

    load_memory.wait()

    def along_z(buf, base, k):
        piece = buf.at[groups[k]]
        send(piece, piece, column_send.at[base + k], column_recv.at[base + k], pairs[k])

    def along_z_next(buf, base, k):
        wait_bytes(buf.at[pl.ds(0, 64 << (k - 1))], column_recv.at[base + k - 1])
        along_z(buf, base, k)

    along_z(slots, 0, 0)
    send(slots.at[here], feats.at[rows((lax.div(turn_to[0], 8) * 8 + reversed_bits(lax.rem(turn_to[0], 8))) * 64, 64)], turn_send.at[0], turn_recv.at[0], turn_to)

    def weight_columns():
        wait_bytes(feats.at[pl.ds(0, 64)], turn_recv.at[0])
        along_z(feats, 3, 0)

    def far_weights(h):
        columns = rows(h * HD, HD)
        send(weight_hbm.at[0, low, columns], w_passing.at[h, low], w_send.at[h], w_up.at[h], up)
        send(weight_hbm.at[0, high, columns], w_passing.at[h, high], w_send.at[h], w_down.at[h], down)

    def pass_on(buf, passing, send_sem, up_sem, down_sem, z_sem, h):
        wait_bytes(passing.at[h, low], up_sem.at[h])
        send(passing.at[h, low], buf.at[h, passing_low], send_sem.at[h], z_sem.at[h], up)
        wait_bytes(passing.at[h, high], down_sem.at[h])
        send(passing.at[h, high], buf.at[h, passing_high], send_sem.at[h], z_sem.at[h], down)

    def pass_weights(h):
        pass_on(weights, w_passing, w_send, w_up, w_down, w_z, h)

    def spread(buf, piece, send_sem, behind_sem, rest_sem, h):
        piece = buf.at[h, piece]
        send(piece, piece, send_sem.at[h], behind_sem.at[h], ahead)
        send(piece, piece, send_sem.at[h], rest_sem.at[h], behind)

    def own_weights(h):
        spread(weights, own, wo_send, wo_behind, w_rest, h)

    def columns_across(buf, base, k):
        wait_bytes(buf.at[pl.ds(0, 256)], column_recv.at[base + 2])
        for device in along_x:
            send(buf.at[column], buf.at[column], x_send.at[k], x_recv.at[k], device)

    along_z_next(slots, 0, 1)
    for h in range(FIRST):
        far_weights(h)
    for h in range(HEADS):
        load_weight(h).wait()
    for h in range(OWN_AHEAD):
        own_weights(h)
    for h in range(FIRST, SECOND):
        far_weights(h)

    def section_block(buf, section):
        low = (section // 8 * 8 + reversed_bits(section % 8)) * 64
        return buf[low : low + 64, :]

    def weight_features():
        wait_bytes(feats.at[pl.ds(0, 1536)], x_recv.at[1])
        for block in range(16):
            place = block_place(block)
            for half in range(2):
                feat_rows[half * 64 : (half + 1) * 64, place * 128 : (place + 1) * 128] = section_block(
                    feats, (2 * block + half + 8) % 32
                )

    def encode():
        wait_bytes(slots.at[pl.ds(0, 1536)], x_recv.at[0])
        for block in range(16):
            place = block_place(block)
            features = jnp.concatenate([section_block(slots, 2 * block + half) for half in range(2)], axis=0)
            encoded[:, place * 128 : (place + 1) * 128] = features.astype(jnp.float32).T.astype(jnp.bfloat16)
        scale_cols_one[...] = jnp.zeros((128, 128), jnp.float32)
        scale_cols_two[...] = jnp.zeros((128, 128), jnp.float32)
        scale_cols_one[0:16, :] = scales_one_ref[0]
        scale_cols_two[0:16, :] = scales_two_ref[0]
        scale_cols_one[...] = scale_cols_one[...].T
        scale_cols_two[...] = scale_cols_two[...].T
        new_cols_one[...] = jnp.zeros((128, 128), jnp.float32)
        new_cols_two[...] = jnp.zeros((128, 128), jnp.float32)
        terms[...] = jnp.zeros((2048, 128), jnp.float32)
        for load in loads:
            load.wait()

    def relay(buf, piece, send_sem, behind_sem, rest_sem, h):
        wait_bytes(buf.at[h, pl.ds(0, 128)], behind_sem.at[h])
        piece = buf.at[h, piece]
        send(piece, piece, send_sem.at[h], rest_sem.at[h], ahead)

    def to_sibling(buf, half, count, send_sem, rest_sem, core_sem, h):
        wait_bytes(buf.at[h, pl.ds(0, count)], rest_sem.at[h])
        piece = buf.at[h, half]
        send(piece, piece, send_sem.at[h], core_sem.at[h], sibling)

    def key_gradient(h):
        wait_bytes(weights.at[h, pl.ds(0, 1024)], w_core.at[h])
        columns = rows(h * HD, HD)
        head_queries = queries_ref[0, :, columns]
        key_rows = dot(encoded[...], weights[h]).astype(jnp.bfloat16)
        expon = jnp.exp(dot(key_rows, head_queries, NT) * SCALE)
        probs = expon / jnp.sum(expon, axis=0, keepdims=True)
        prob_grad = dot(values_ref[0, :, columns], out_grad_ref[0, :, columns], NT)
        score_grad = probs * (prob_grad - jnp.sum(probs * prob_grad, axis=0, keepdims=True)) * SCALE
        key_grad = dot(score_grad.astype(jnp.bfloat16), head_queries).astype(jnp.bfloat16)
        grads[h, own, :] = key_grad
        send(grads.at[h, own_low], g_passing.at[h, low], g_send.at[h], g_up.at[h], up)
        send(grads.at[h, own_high], g_passing.at[h, high], g_send.at[h], g_down.at[h], down)
        spread(grads, own, g_send, go_behind, go_rest, h)
        terms[...] += dot(weights[h], key_grad, NT)

    lane = lax.broadcasted_iota(jnp.int32, (128, 128), 1)

    def adam(h):
        wait_bytes(grads.at[h, pl.ds(0, 512)], go_core.at[h])
        wait_bytes(grads.at[h, pl.ds(0, 512)], g_core.at[h])
        weight_grad = dot(feat_rows[...], grads[h])
        for part in range(HD // 128):
            block = h * (HD // 128) + part
            columns = rows(block * 128, 128)
            grad = weight_grad[:, part * 128 : (part + 1) * 128]
            chosen = lane == block
            scale_one = jnp.sum(jnp.where(chosen, scale_cols_one[...], 0.0), axis=1, keepdims=True)
            scale_two = jnp.sum(jnp.where(chosen, scale_cols_two[...], 0.0), axis=1, keepdims=True)
            first_prev = codes_one_ref[0, :, columns].astype(jnp.float32) * scale_one
            second_prev = codes_two_ref[0, :, columns].astype(jnp.float32) * scale_two
            first = beta_one * first_prev + (1.0 - beta_one) * grad
            second = beta_two * second_prev + (1.0 - beta_two) * grad * grad
            update = first / corr_one / (jnp.sqrt(second / corr_two) + 1e-08)
            first_max = jnp.max(jnp.abs(first), axis=1, keepdims=True) + 1e-06
            second_max = jnp.max(second, axis=1, keepdims=True) + 1e-06
            update_ref[0, :, columns] = update.astype(jnp.bfloat16)
            new_one_ref[0, :, columns] = (first / first_max).astype(jnp.bfloat16)
            new_two_ref[0, :, columns] = (second / second_max).astype(jnp.bfloat16)
            new_cols_one[...] = jnp.where(chosen, first_max, new_cols_one[...])
            new_cols_two[...] = jnp.where(chosen, second_max, new_cols_two[...])

    def memory_terms():
        for block in range(16):
            place = block_place(block)
            halves_out[block * 128 : (block + 1) * 128, :] = (
                terms[place * 128 : (place + 1) * 128, :].astype(jnp.bfloat16)
            )
        for k, device in zip((1, 3, 2), along_x):
            part = rows(lax.rem(x + k, 4) * 512, 512)
            send(halves_out.at[part], halves_in.at[k - 1], half_send.at[0], half_recv.at[0], device)

    def exchange_parts(k):
        size = 256 >> k
        low = rows(other_blocks[k] * size, size)
        parts_out[low, :] = totals[low, :].astype(jnp.bfloat16)
        landing = parts_in.at[pl.ds(512 - 2 * size, size)]
        send(parts_out.at[low], landing, part_send.at[k], part_recv.at[k], pairs[2 - k])

    def add_parts(k):
        size = 256 >> k
        landing = pl.ds(512 - 2 * size, size)
        wait_bytes(parts_in.at[landing], part_recv.at[k])
        low = rows(kept_blocks[k] * size, size)
        totals[low, :] += parts_in[landing, :].astype(jnp.float32)

    kept_blocks = [unit_bit, unit_bit * 2 + quarter_bit, place]
    other_blocks = [1 - unit_bit, unit_bit * 2 + 1 - quarter_bit, unit_bit * 4 + quarter_bit * 2 + 1 - half_bit]

    def memory_columns():
        wait_bytes(halves_out.at[pl.ds(0, 1536)], half_recv.at[0])
        total = halves_out[column, :].astype(jnp.float32)
        for k in range(3):
            total += halves_in[k].astype(jnp.float32)
        for z in range(8):
            low = reversed_bits(z) * 64
            totals[low : low + 64, :] = total[z * 64 : (z + 1) * 64, :]
        exchange_parts(0)

    def memory_parts(k):
        add_parts(k)
        exchange_parts(k + 1)

    def memory_result():
        add_parts(2)
        memory_grad_ref[...] = totals[rows(place * 64, 64), :]

    def far_gradient(h):
        wait_bytes(grads.at[h, pl.ds(0, 128)], g_z.at[h])
        piece = grads.at[h, other]
        for device in (ahead, behind, opposite):
            send(piece, piece, g_send.at[h], g_rest.at[h], device)

    def far_range(first, last):
        for h in range(first, last):
            far_weights(h)

    def step(t, _):
        def at(first, count, act):
            @pl.when((t >= first) & (t < first + count))
            def _():
                act(t - first)

        k, g = KEY_LAG, GRAD_LAG
        f = FAR_LAG
        at(0, HEADS - 2, lambda h: pass_weights(h + 2))
        at(g, HEADS, lambda h: pass_on(grads, g_passing, g_send, g_up, g_down, g_z, h))
        at(f, HEADS, lambda h: spread_far(weights, w_send, w_z, w_behind, w_rest, h))
        at(0, HEADS - OWN_AHEAD, lambda h: own_weights(h + OWN_AHEAD))
        at(0, 1, lambda h: along_z_next(slots, 0, 2))
        at(0, 1, lambda h: weight_columns())
        at(2, 1, lambda h: along_z_next(feats, 3, 1))
        at(0, 1, lambda h: far_range(SECOND, THIRD))
        at(1, 1, lambda h: columns_across(slots, 0, 0))
        at(4, 1, lambda h: along_z_next(feats, 3, 2))
        at(1, 1, lambda h: far_range(THIRD, HEADS))
        at(6, 1, lambda h: columns_across(feats, 3, 1))
        at(0, HEADS, lambda h: relay(weights, own_behind, w_send, wo_behind, w_rest, h))
        at(f + 1, HEADS, lambda h: relay(weights, other_behind, w_send, w_behind, w_rest, h))
        at(f + 2, HEADS, lambda h: to_sibling(weights, mine, 512, w_send, w_rest, w_core, h))
        at(k, 1, lambda h: encode())
        at(k, HEADS, key_gradient)
        at(k + HEADS - 1, 1, lambda h: memory_terms())
        at(k + 1, HEADS, lambda h: relay(grads, own_behind, g_send, go_behind, go_rest, h))
        at(k + 2, HEADS, lambda h: to_sibling(grads, own_half, 256, g_send, go_rest, go_core, h))
        at(g + f, HEADS, far_gradient)
        at(g + f + 1, HEADS, lambda h: to_sibling(grads, other_half, 384, g_send, g_rest, g_core, h))
        at(g + f + 2, 1, lambda h: weight_features())
        at(g + f + 2, HEADS, adam)
        at(k + HEADS + 1, 1, lambda h: memory_columns())
        at(k + HEADS + 2, 1, lambda h: memory_parts(0))
        at(k + HEADS + 3, 1, lambda h: memory_parts(1))
        at(k + HEADS + 4, 1, lambda h: memory_result())
        return 0

    def spread_far(buf, send_sem, z_sem, behind_sem, rest_sem, h):
        wait_bytes(buf.at[h, pl.ds(0, 128)], z_sem.at[h])
        spread(buf, other, send_sem, behind_sem, rest_sem, h)

    pass_weights(0)
    pass_weights(1)
    lax.fori_loop(0, GRAD_LAG + FAR_LAG + HEADS + 2, step, 0)
    new_scale_one_ref[0] = new_cols_one[...].T[0:16, :]
    new_scale_two_ref[0] = new_cols_two[...].T[0:16, :]

    def sent(h, _):
        wait_bytes(weights.at[h, pl.ds(0, 1792)], w_send.at[h])
        wait_bytes(weights.at[h, pl.ds(0, 256)], wo_send.at[h])
        wait_bytes(grads.at[h, pl.ds(0, 2048)], g_send.at[h])
        return 0

    lax.fori_loop(0, HEADS, sent, 0)
    wait_bytes(slots.at[pl.ds(0, 64)], turn_send.at[0])
    wait_bytes(slots.at[pl.ds(0, 1536)], x_send.at[0])
    wait_bytes(slots.at[pl.ds(0, 1536)], x_send.at[1])
    for k in range(3):
        wait_bytes(slots.at[pl.ds(0, 64 << k)], column_send.at[k])
        wait_bytes(slots.at[pl.ds(0, 64 << k)], column_send.at[3 + k])
        wait_bytes(parts_out.at[pl.ds(0, 256 >> k)], part_send.at[k])
    wait_bytes(halves_out.at[pl.ds(0, 1536)], half_send.at[0])


def local(memory, queries, values, out_grad, key_weight, codes_one, scales_one, codes_two, scales_two):
    bf16, f32 = jnp.bfloat16, jnp.float32
    vmem, anywhere = pl.BlockSpec(memory_space=pltpu.VMEM), pl.BlockSpec(memory_space=pl.ANY)
    sems = pltpu.SemaphoreType.DMA
    one, each = sems((1,)), sems((HEADS,))
    shapes = (
        jax.ShapeDtypeStruct((64, 128), f32),
        jax.ShapeDtypeStruct((1, 128, 2048), bf16),
        jax.ShapeDtypeStruct((1, 128, 2048), bf16),
        jax.ShapeDtypeStruct((1, 16, 128), f32),
        jax.ShapeDtypeStruct((1, 128, 2048), bf16),
        jax.ShapeDtypeStruct((1, 16, 128), f32),
    )
    outs = pl.pallas_call(
        kernel,
        out_shape=shapes,
        in_specs=[anywhere] * 6 + [vmem, anywhere, vmem],
        out_specs=(vmem,) * 6,
        scratch_shapes=[pltpu.VMEM((1, 128, 2048), bf16)] * 5
        + [
            pltpu.VMEM((HEADS, 2048, HD), bf16),
            pltpu.VMEM((HEADS, 2048, HD), bf16),
            pltpu.VMEM((HEADS, 128, HD), bf16),
            pltpu.VMEM((HEADS, 128, HD), bf16),
            pltpu.VMEM((2048, 128), bf16),
            pltpu.VMEM((2048, 128), bf16),
            pltpu.VMEM((128, 2048), bf16),
            pltpu.VMEM((128, 2048), bf16),
            pltpu.VMEM((2048, 128), f32),
            pltpu.VMEM((2048, 128), bf16),
            pltpu.VMEM((3, 512, 128), bf16),
            pltpu.VMEM((512, 128), f32),
            pltpu.VMEM((512, 128), bf16),
            pltpu.VMEM((512, 128), bf16),
        ]
        + [pltpu.VMEM((128, 128), f32)] * 4
        + [sems((6 + HEADS,)), one, one, sems((6,)), sems((6,)), sems((2,)), sems((2,)), one, one, sems((3,)), sems((3,))]
        + [each] * 7
        + [each] * 11,
        compiler_params=pltpu.CompilerParams(
            collective_id=0, has_side_effects=True, vmem_limit_bytes=56 << 20
        ),
        name="projection_backward",
    )(memory.T, queries, values, out_grad, key_weight, codes_one, scales_one, codes_two, scales_two)
    outs = pl.pallas_call(
        writer,
        out_shape=shapes,
        in_specs=[vmem] * 6,
        out_specs=(anywhere,) * 6,
        scratch_shapes=[sems((6,))],
        name="write_results",
    )(*outs)
    return (outs[0].T, *outs[1:])


def solution(mesh):
    return jax.shard_map(
        local,
        mesh=mesh,
        in_specs=(
            P("dp", "section"),
            P("section", "dp", None),
            P("section", "dp", None),
            P("section", "dp", None),
            P("section", "dp", None),
            P("section", "dp", None),
            P("section", None, "dp"),
            P("section", "dp", None),
            P("section", None, "dp"),
        ),
        out_specs=(
            P("dp", "section"),
            P("section", "dp", None),
            P("section", "dp", None),
            P("section", None, "dp"),
            P("section", "dp", None),
            P("section", None, "dp"),
        ),
        check_vma=False,
    )
```
